256 devices in a mesh: replica: 4 (over x_hi, core), fsdp: 8 (over y, x_lo), tensor: 8 (over z).
Axes of the slice: x: 4 (x_hi: 2, x_lo: 2; x = x_hi * 2 + x_lo), y: 4, z: 8, core: 2. Of those that a mesh axis runs over, the one named last changes fastest.
Arguments:
- partials: bfloat16 [4, 4, 4096, 8192], P('replica', None, 'fsdp', 'tensor'), may hold values from -0.375 to 0.375
- factor_in: float32 [4, 8, 5, 1024, 1024], P('replica', 'tensor', None, None, 'fsdp'), may hold values from -6 to 6
Outputs:
- factor_out: float32 [4, 8, 5, 1024, 1024], P('replica', 'tensor', None, None, 'fsdp')
The draws below stay inside these ranges and needn't reach their ends.
All inputs are finite; a program needn't handle non-finite values.
Results may differ from the reference program's by a relative error of at most 0.0035.
Values may be sent and summed in bfloat16 or wider, within the bound.
No kernel may reach another device: no remote copies, remote signals or barrier semaphores. Data moves between devices by JAX's collectives and lax.ppermute only.
A program may use at most 128 MiB of HBM per device.

```python
import jax
import jax.numpy as jnp
from jax import lax

M = 4096
N = 8192
LAYERS = 4
NB = 8
BS = 1024
H = 5
N_REPLICA = 4


def with_spikes(values, stream_key, source, target, parts, factor):
    def block_of(dim):
        return (jnp.arange(values.shape[dim]) // (values.shape[dim] // parts)).reshape((-1,) + (1,) * (values.ndim - 1 - dim))

    near = jax.random.permutation(stream_key, parts)[block_of(target)]
    other_side = (block_of(target) + parts // 2) % parts
    return jnp.where((block_of(source) == near) | (block_of(source) == other_side), factor * values, values)


def shard_levels(stream_key, extent, split, low, largest):
    factor_of = 1.0
    for dim, shards_of in split:
        heights = jax.random.uniform(jax.random.fold_in(jax.random.fold_in(stream_key, 6), dim), (shards_of,), jnp.float32, low / len(split), largest / len(split))
        factor_of = factor_of * jnp.repeat(jnp.exp(heights), extent[dim] // shards_of).reshape((-1,) + (1,) * (len(extent) - 1 - dim))
    return factor_of


def gaussian(rng, dims, width, most, shards=(), dtype=jnp.bfloat16):
    level = shard_levels(rng, dims, shards, -0.22, 0.18) if shards else 1.0
    array = jax.random.normal(rng, dims, jnp.float32) * width * level
    return jnp.minimum(jnp.maximum(array, -most), most).astype(dtype)


def noise_with(own_key, dims, spread, reach, cuts, heavy, dtype=jnp.bfloat16):
    entries = spread * jax.random.normal(own_key, dims, jnp.float32)
    if cuts:
        entries = entries * shard_levels(own_key, dims, cuts, -0.22, 0.18)
    return jnp.clip(with_spikes(entries, jax.random.fold_in(own_key, 3), *heavy), -reach, reach).astype(dtype)


def setup_inputs(seed: int = 0) -> dict:
    seeds = jax.random.split(jax.random.key(seed), 3)
    return {
        "partials": noise_with(seeds[0], (N_REPLICA, LAYERS, M, N), (0.5 * M ** -0.25), 0.375, ((0, 4), (2, 8), (3, 8)), (0, 1, 4, 2.0)),
        "factor_in": gaussian(seeds[1], (LAYERS, NB, H, BS, BS), 1.0, 6.0, ((0, 4), (1, 8), (4, 8)), jnp.float32),
    }


def reference(partials, factor_in):
    def one_layer(args):
        layer_parts, layer_factor = args
        grad = jnp.sum(layer_parts.astype(jnp.float32), axis=0).astype(jnp.bfloat16)
        blocks = grad.reshape(M, NB, BS).astype(jnp.float32)
        pieces = []
        for step in range(H):
            other = jnp.roll(blocks, step, axis=1)
            pieces.append(jnp.einsum("mib,mic->ibc", blocks, other, precision=lax.Precision.HIGHEST))
        gram = jnp.stack(pieces, axis=1)
        return 0.9 * layer_factor + 0.1 * gram
    return lax.map(one_layer, (jnp.moveaxis(partials, 1, 0), factor_in))
```

```python
import jax
import jax.numpy as jnp
from jax import lax
from jax.experimental import pallas as pl
from jax.experimental.pallas import tpu as pltpu
from jax.sharding import PartitionSpec as P

DIMS = (2, 2, 4, 2, 8)
AXES = ("replica", "fsdp", "tensor")
VMEM = 48 * 1024 * 1024


def index_of(xh, core, y, xl, z):
    return (((xh * 2 + core) * 4 + y % 4) * 2 + xl) * 8 + z % 8


def pairs(move):
    out = []
    for xh in range(2):
        for core in range(2):
            for y in range(4):
                for xl in range(2):
                    for z in range(8):
                        out.append((index_of(xh, core, y, xl, z), index_of(*move(xh, core, y, xl, z))))
    return out


def along_x(by):
    def move(xh, core, y, xl, z):
        x = (2 * xh + xl + by) % 4
        return x // 2, core, y, x % 2, z
    return pairs(move)


def along_y(by):
    return pairs(lambda xh, core, y, xl, z: (xh, core, y + by, xl, z))


def along_z(by):
    return pairs(lambda xh, core, y, xl, z: (xh, core, y, xl, z + by))


def to_owner(by):
    return pairs(lambda xh, core, y, xl, z: (xh, xl, y, core, z + by))


SIBLING = pairs(lambda xh, core, y, xl, z: (xh, 1 - core, y, xl, z))


def send(value, where):
    return lax.ppermute(value, AXES, where)


def call(body, grid, ins, outs, shapes, flops=0):
    bytes_accessed = sum(s.size * s.dtype.itemsize for s in jax.tree.leaves(shapes)) * 2
    return pl.pallas_call(
        body,
        grid_spec=pltpu.PrefetchScalarGridSpec(num_scalar_prefetch=1, grid=grid, in_specs=ins, out_specs=outs),
        out_shape=shapes,
        compiler_params=pltpu.CompilerParams(vmem_limit_bytes=VMEM),
        cost_estimate=pl.CostEstimate(flops=flops, bytes_accessed=bytes_accessed, transcendentals=0),
    )


def other_half(partials, where):
    layers, rows, columns = partials.shape

    def body(where_ref, x_ref, o_ref):
        o_ref[...] = x_ref[...]

    return call(
        body, (4,),
        [pl.BlockSpec((layers, rows, 128), lambda q, w: (0, 0, 2 * q + 1 - w[0]))],
        pl.BlockSpec((layers, rows, 128), lambda q, w: (0, 0, q)),
        jax.ShapeDtypeStruct((layers, rows, columns // 2), partials.dtype),
    )(where, partials)


def pair_sums(partials, got, where):
    _, rows, columns = partials.shape

    def body(where_ref, *refs):
        for k in range(3):
            total = refs[2 * k][0].astype(jnp.float32) + refs[2 * k + 1][0].astype(jnp.float32)
            refs[6 + k][...] = total.astype(jnp.bfloat16)

    ins = []
    for k in (1, 2, 3):
        ins.append(pl.BlockSpec((1, rows, 128), lambda q, w, k=k: (lax.rem(w[1] + k, 4), 0, 2 * q + w[0])))
        ins.append(pl.BlockSpec((1, rows, 128), lambda q, w, k=k: (lax.rem(w[1] + k, 4), 0, q)))
    return call(
        body, (4,), ins,
        [pl.BlockSpec((rows, 128), lambda q, w: (0, q))] * 3,
        [jax.ShapeDtypeStruct((rows, columns // 2), jnp.bfloat16)] * 3,
    )(where, *[partials, got] * 3)


def gradient(partials, got, second, left, right, where):
    _, rows, columns = partials.shape

    def body(where_ref, own_ref, got_ref, second_ref, left_ref, right_ref, plain_ref, turned_ref):
        f32 = jnp.float32
        near = own_ref[0].astype(f32) + got_ref[0].astype(f32) + second_ref[...].astype(f32)
        far = left_ref[...].astype(f32) + right_ref[...].astype(f32)
        near, far = near.astype(jnp.bfloat16), far.astype(jnp.bfloat16)
        plain_ref[:rows] = near
        plain_ref[rows:] = far
        turned_ref[:rows] = near
        turned_ref[rows:] = far

    shape = jax.ShapeDtypeStruct((2 * rows, columns // 2), jnp.bfloat16)
    half = pl.BlockSpec((rows, 128), lambda q, w: (0, q))
    return call(
        body, (4,),
        [
            pl.BlockSpec((1, rows, 128), lambda q, w: (w[1], 0, 2 * q + w[0])),
            pl.BlockSpec((1, rows, 128), lambda q, w: (w[1], 0, q)),
            half, half, half,
        ],
        [
            pl.BlockSpec((2 * rows, 128), lambda q, w: (0, q)),
            pl.BlockSpec((2 * rows, 128), lambda q, w: (0, lax.rem(q + 4 - w[2], 4))),
        ],
        [shape, shape],
    )(where, partials, got, second, left, right)


def product(mine, sibling, block, where):
    depth, width = mine.shape

    def body(where_ref, mine_ref, sibling_ref, block_ref, own_ref, *part_refs):
        for k, ref in enumerate((mine_ref, sibling_ref)):
            half = lax.rem(where_ref[0] + k, 2)
            terms = lax.dot_general(ref[...], block_ref[...], (((0,), (0,)), ((), ())), preferred_element_type=jnp.float32)
            for q in range(4):
                rows = pl.ds(pl.multiple_of((2 * q + half) * 128, 128), 128)
                own_ref[rows, :] = terms[q * 128:(q + 1) * 128, :128]
                for j, part_ref in enumerate(part_refs):
                    part_ref[rows, :] = terms[q * 128:(q + 1) * 128, (j + 1) * 128:(j + 2) * 128].astype(jnp.bfloat16)

    whole = pl.BlockSpec((depth, width), lambda i, w: (0, 0))
    part = pl.BlockSpec((2 * width, 128), lambda i, w: (0, 0))
    return call(
        body, (1,),
        [whole, whole, whole],
        [part] * 4,
        [jax.ShapeDtypeStruct((2 * width, 128), jnp.float32)] + [jax.ShapeDtypeStruct((2 * width, 128), jnp.bfloat16)] * 3,
        flops=4 * depth * width * width,
    )(where, mine, sibling, block)


def sum_over_y(parts):
    def joined(j):
        return parts[0][j] if len(parts) == 1 else jnp.concatenate([p[j] for p in parts])

    got = [send(joined(j), along_y(j)) for j in (1, 2, 3)]
    rows = parts[0][0].shape[0]
    sums = []
    for n, part in enumerate(parts):
        total = part[0]
        for piece in got:
            total = total + piece[n * rows:(n + 1) * rows].astype(jnp.float32)
        sums.append(total)
    return sums


def per_device(partials, factor_in):
    replica, fsdp = lax.axis_index("replica"), lax.axis_index("fsdp")
    core, y = replica % 2, fsdp // 2
    x = 2 * (replica // 2) + fsdp % 2
    where = jnp.stack([core, x, y]).astype(jnp.int32)
    partials = partials[0]

    got = send(other_half(partials, where), SIBLING)
    one, two, three = pair_sums(partials, got, where)
    left, second, right = send(one, along_x(1)), send(two, along_x(2)), send(three, along_x(3))
    plain, turned = gradient(partials, got, second, left, right, where)

    up1 = send(turned, along_z(1))
    down1 = send(plain, along_z(-1))
    plain_s = send(plain, SIBLING)
    r0, = sum_over_y([product(plain, plain_s, turned, where)])
    up2 = send(up1, along_z(1))
    down2 = send(down1, along_z(-1))
    down1_s = send(down1, SIBLING)
    r1, r2 = sum_over_y([product(plain, plain_s, up1, where), product(down1, down1_s, up1, where)])
    down2_s = send(down2, SIBLING)
    r3, r4 = sum_over_y([product(down1, down1_s, up2, where), product(down2, down2_s, up2, where)])
    near = send(jnp.concatenate([r0, r1]), to_owner(0))
    grams = [near[:1024], near[1024:], send(r2, to_owner(1)), send(r3, to_owner(1)), send(r4, to_owner(2))]
    return 0.9 * factor_in + 0.1 * jnp.stack(grams)[None, None]


def solution(mesh):
    placed = (P("replica", None, "fsdp", "tensor"), P("replica", "tensor", None, None, "fsdp"))
    return jax.shard_map(
        per_device,
        mesh=mesh,
        in_specs=placed,
        out_specs=P("replica", "tensor", None, None, "fsdp"),
        check_vma=False,
    )
```
